1024 devices in a mesh: dom: 128 (over z, x), repl: 8 (over y, core).
Axes of the slice: x: 4, y: 4, z: 32, core: 2. Of those that a mesh axis runs over, the one named last changes fastest.
Arguments:
- features: bfloat16 [262144, 128], P(('dom', 'repl')), may hold values from -6 to 6
- weight: bfloat16 [128, 128], replicated, may hold values from -0.5 to 0.5
- grad_out: bfloat16 [262144, 128], P(('dom', 'repl')), may hold values from -6 to 6
- tile_values: bfloat16 [128, 8, 24, 256, 256], P('dom', 'repl'), may hold values from -0.09375 to 0.09375
- tile_rows: int32 [128, 8, 24], P('dom', 'repl'), may hold values from 0 to 7
- tile_cols: int32 [128, 8, 24], P('dom', 'repl'), may hold values from 0 to 4
- tile_count: int32 [128, 8], P('dom', 'repl'), may hold values from 1 to 24, as said below
Outputs:
- projected: bfloat16 [262144, 128], P(('dom', 'repl'))
- grad_features: bfloat16 [262144, 128], P(('dom', 'repl'))
The draws below stay inside these ranges and needn't reach their ends.
Inputs may be any that keep to these rules, and one draw needn't show every extreme that they name: `tile_count`: some device has all 24 slots live.
All inputs are finite; a program needn't handle non-finite values.
Results may differ from the reference program's by a relative error of at most 0.017.
Values may be sent and summed in bfloat16 or wider, within the bound.
No kernel may reach another device: no remote copies, remote signals or barrier semaphores. Data moves between devices by JAX's collectives and lax.ppermute only.
A program may use at most 32 MiB of HBM per device.

```python
import jax
import jax.numpy as jnp
from jax import lax

FEAT = 128
TILE = 256
TILES_DEV = 24
REACH = 2
NODES = 262144
N_DOM = 128
N_REPL = 8


def draw_tile_count(key, part):
    key = jax.random.fold_in(key, 7)
    key_base, key_heavy, key_high, key_spot = jax.random.split(key, 4)
    base_counts = jax.random.randint(key_base, (N_DOM, N_REPL), 1, TILES_DEV // 3 + 1)
    heavy_flag = jax.random.randint(key_heavy, (N_DOM, N_REPL), 0, 8) == 0
    high_counts = jax.random.randint(key_high, (N_DOM, N_REPL), TILES_DEV // 2, TILES_DEV + 1)
    counts = jnp.where(heavy_flag, high_counts, base_counts).reshape(N_DOM * N_REPL)
    chosen_spot = jax.random.randint(key_spot, (), 0, N_DOM * N_REPL)
    counts = jnp.where(jnp.arange(N_DOM * N_REPL) == chosen_spot, TILES_DEV, counts)
    return counts.reshape(N_DOM, N_REPL).astype(jnp.int32)


def place_ends(array, rng, smallest, top_value):
    longest = array.shape.index(max(array.shape))
    spots = []
    for shift in (0, 1):
        where = [jax.random.randint(jax.random.fold_in(rng, axis), (), 0, length) for axis, length in enumerate(array.shape)]
        where[longest] = (where[longest] + shift) % array.shape[longest]
        spots.append(tuple(where))
    return array.at[spots[0]].set(smallest).at[spots[1]].set(top_value)


def block_scale(rng, shape, shards, least, high):
    def one(position, shards_of):
        draws = jax.random.uniform(jax.random.fold_in(jax.random.fold_in(rng, 6), position), (shards_of,), jnp.float32, least / len(shards), high / len(shards))
        return jnp.repeat(jnp.exp(draws), shape[position] // shards_of).reshape((-1,) + (1,) * (len(shape) - position - 1))

    loudness = one(*shards[0])
    for cut in shards[1:]:
        loudness = loudness * one(*cut)
    return loudness


def gaussian(stream_key, dims, scale, limit, pieces=(), held_as=jnp.bfloat16):
    result = jax.random.normal(stream_key, dims, jnp.float32) * scale
    if len(pieces) > 0:
        result = block_scale(stream_key, dims, pieces, -0.22, 0.18) * result
    return jnp.clip(result, min=-limit, max=limit).astype(held_as)


def setup_inputs(seed: int = 0) -> dict:
    arg_keys = jax.random.split(jax.random.key(seed), 8)
    return {
        "features": gaussian(arg_keys[0], (NODES, FEAT), 1.0, 6.0, ((0, 1024),)),
        "weight": gaussian(arg_keys[1], (FEAT, FEAT), FEAT ** -0.5, 0.5),
        "grad_out": gaussian(arg_keys[2], (NODES, FEAT), 1.0, 6.0, ((0, 1024),)),
        "tile_values": gaussian(arg_keys[3], (N_DOM, N_REPL, TILES_DEV, TILE, TILE), 0.015625, 0.09375, ((0, 128), (1, 8))),
        "tile_rows": place_ends(jax.random.randint(arg_keys[4], (N_DOM, N_REPL, TILES_DEV), 0, N_REPL), jax.random.fold_in(arg_keys[4], 1), 0, N_REPL - 1).astype(jnp.int32),
        "tile_cols": place_ends(jax.random.randint(arg_keys[5], (N_DOM, N_REPL, TILES_DEV), 0, 2 * REACH + 1), jax.random.fold_in(arg_keys[5], 1), 0, 2 * REACH).astype(jnp.int32),
        "tile_count": draw_tile_count(jax.random.fold_in(arg_keys[7], 71), 0),
    }


def pick_blocks(candidates, chosen):
    return jnp.take(candidates, chosen, axis=0)


def reference(features, weight, grad_out, tile_values, tile_rows, tile_cols, tile_count):
    spread = 2 * REACH + 1
    slot_ids = jnp.arange(TILES_DEV, dtype=jnp.int32)
    is_live = slot_ids[None, None, :] < tile_count[:, :, None]
    block_ids = jnp.arange(N_REPL, dtype=jnp.int32)
    offset_ids = jnp.arange(spread, dtype=jnp.int32)
    row_onehot = jnp.where((tile_rows[:, :, None, :] == block_ids[None, None, :, None]) & is_live[:, :, None, :], 1.0, 0.0).astype(jnp.float32)
    col_onehot = jnp.where((tile_cols[:, :, None, :] == offset_ids[None, None, :, None]) & is_live[:, :, None, :], 1.0, 0.0).astype(jnp.float32)
    feature_blocks = features.astype(jnp.float32).reshape(N_DOM, N_REPL, TILE, FEAT)
    margin_zeros = jnp.zeros((REACH, N_REPL, TILE, FEAT), jnp.float32)
    padded = jnp.concatenate([margin_zeros, feature_blocks, margin_zeros], axis=0)
    slab_ids = jnp.arange(N_DOM, dtype=jnp.int32)

    def slab_forward(slab_index):
        nearby = jnp.swapaxes(lax.dynamic_slice_in_dim(padded, slab_index, spread, 0), 0, 1)
        gathered = jax.vmap(pick_blocks)(nearby, tile_cols[slab_index])
        values = tile_values[slab_index].astype(jnp.float32)
        products = jnp.einsum("rsij,rsjf->rsif", values, gathered, precision=lax.Precision.HIGHEST)
        partial_value = jnp.einsum("rbs,rsif->rbif", row_onehot[slab_index], products, precision=lax.Precision.HIGHEST)
        rounded = lax.optimization_barrier(partial_value.astype(jnp.bfloat16)).astype(jnp.float32)
        return jnp.sum(rounded, axis=0)

    hidden = lax.map(slab_forward, slab_ids).reshape(NODES, FEAT).astype(jnp.bfloat16)
    projected = jnp.dot(hidden, weight, preferred_element_type=jnp.float32).astype(jnp.bfloat16)

    grad_hidden = jnp.dot(grad_out, weight.T, preferred_element_type=jnp.float32).astype(jnp.bfloat16)
    grad_blocks = grad_hidden.astype(jnp.float32).reshape(N_DOM, N_REPL, TILE, FEAT)

    def slab_backward(running, slab_index):
        slab_grads = grad_blocks[slab_index]
        grad_tiles = jnp.take(slab_grads, tile_rows[slab_index], axis=0)
        values = tile_values[slab_index].astype(jnp.float32)
        backward_terms = jnp.einsum("rsij,rsif->rsjf", values, grad_tiles, precision=lax.Precision.HIGHEST)
        offset_terms = jnp.einsum("rws,rsjf->wrjf", col_onehot[slab_index], backward_terms, precision=lax.Precision.HIGHEST)
        current = lax.dynamic_slice_in_dim(running, slab_index, spread, 0)
        running = lax.dynamic_update_slice_in_dim(running, current + offset_terms, slab_index, 0)
        return running, None

    start_sums = jnp.zeros((N_DOM + 2 * REACH, N_REPL, TILE, FEAT), jnp.float32)
    running, unused = lax.scan(slab_backward, start_sums, slab_ids)
    grad_features = running[REACH:REACH + N_DOM].reshape(NODES, FEAT).astype(jnp.bfloat16)
    return projected, grad_features
```

```python
import functools

import jax
import jax.numpy as jnp
from jax import lax
from jax.experimental import pallas as pl
from jax.experimental.pallas import tpu as pltpu
from jax.sharding import PartitionSpec as P

REACH = 2
SPREAD = 2 * REACH + 1


def shifted(array, axis, by):
    devices = lax.axis_size(axis)
    pairs = [(i, i + by) for i in range(devices) if 0 <= i + by < devices]
    return lax.ppermute(array, axis, pairs)


def forward_kernel(rows, cols, count, tiles, f0, f1, f2, f3, f4, out, held, near, total, sems):
    live = count[0]
    slots = held.shape[0]

    def fetch(slot):
        return pltpu.make_async_copy(tiles.at[slot], held.at[slot], sems.at[slot])

    @pl.loop(0, live)
    def _(slot):
        fetch(slot).start()

    for offset, ref in enumerate((f0, f1, f2, f3, f4)):
        near[offset] = ref[...]
    total[...] = jnp.zeros_like(total)

    @pl.loop(0, live)
    def _(slot):
        fetch(slot).wait()
        row = rows[slot]
        total[row] += jnp.dot(held[slot], near[cols[slot]], preferred_element_type=jnp.float32)

    out[...] = total[...].astype(out.dtype)


def backward_kernel(rows, cols, count, tiles, grads, c0, c1, c2, c3, c4, held, turned, total, sems):
    live = count[0]

    def fetch(slot):
        return pltpu.make_async_copy(tiles.at[slot], held.at[slot], sems.at[slot])

    @pl.loop(0, live)
    def _(slot):
        fetch(slot).start()

    for block in range(grads.shape[0]):
        turned[block] = grads[block].T
    total[...] = jnp.zeros_like(total)

    @pl.loop(0, live)
    def _(slot):
        fetch(slot).wait()
        col = cols[slot]
        total[col] += jnp.dot(turned[rows[slot]], held[slot], preferred_element_type=jnp.float32)

    for offset, ref in enumerate((c0, c1, c2, c3, c4)):
        ref[...] = total[offset].T.astype(ref.dtype)


def project_kernel(parts, weight, out):
    total = jnp.sum(parts[...].astype(jnp.float32), axis=0)
    out[...] = jnp.dot(
        total.astype(jnp.bfloat16), weight[...], preferred_element_type=jnp.float32
    ).astype(out.dtype)


def features_kernel(c0, c1, c2, c3, c4, weight, out):
    total = c2[...]
    for ref in (c0, c1, c3, c4):
        total += ref[...].astype(jnp.float32)
    out[...] = lax.dot_general(
        total.astype(jnp.bfloat16),
        weight[...],
        (((1,), (1,)), ((), ())),
        preferred_element_type=jnp.float32,
    ).astype(out.dtype)


SMEM = pl.BlockSpec(memory_space=pltpu.SMEM)
VMEM = pl.BlockSpec(memory_space=pltpu.VMEM)
ANY = pl.BlockSpec(memory_space=pl.ANY)


def body(features, weight, grad_out, tile_values, tile_rows, tile_cols, tile_count):
    slots, edge = tile_values.shape[2], tile_values.shape[3]
    width = features.shape[1]
    blocks = lax.axis_size("repl")
    tiles = tile_values.reshape(slots, edge, edge)
    rows = tile_rows.reshape(slots)
    cols = tile_cols.reshape(slots)
    count = tile_count.reshape(1)
    block = jax.ShapeDtypeStruct((edge, width), jnp.bfloat16)

    spread_grads = jnp.broadcast_to(grad_out[None], (blocks, edge, width))
    slab_grads = lax.all_to_all(spread_grads, "repl", 0, 0, tiled=True)
    near = [
        features if offset == REACH else shifted(features, "dom", REACH - offset)
        for offset in range(SPREAD)
    ]
    flops = 2 * slots * edge * edge * width
    cost = pl.CostEstimate(flops=flops, bytes_accessed=slots * edge * edge * 2, transcendentals=0)
    partial = pl.pallas_call(
        forward_kernel,
        out_shape=jax.ShapeDtypeStruct((blocks, edge, width), jnp.bfloat16),
        in_specs=[SMEM] * 3 + [ANY] + [VMEM] * SPREAD,
        out_specs=VMEM,
        scratch_shapes=[
            pltpu.VMEM((slots, edge, edge), jnp.bfloat16),
            pltpu.VMEM((SPREAD, edge, width), jnp.bfloat16),
            pltpu.VMEM((blocks, edge, width), jnp.float32),
            pltpu.SemaphoreType.DMA((slots,)),
        ],
        cost_estimate=cost,
        name="forward",
    )(rows, cols, count, tiles, *near)
    slab_parts = lax.all_to_all(partial, "repl", 0, 0, tiled=True)
    terms = pl.pallas_call(
        backward_kernel,
        out_shape=[
            jax.ShapeDtypeStruct((edge, width), jnp.float32) if offset == REACH else block
            for offset in range(SPREAD)
        ],
        in_specs=[SMEM] * 3 + [ANY] + [VMEM],
        out_specs=[VMEM] * SPREAD,
        scratch_shapes=[
            pltpu.VMEM((slots, edge, edge), jnp.bfloat16),
            pltpu.VMEM((blocks, width, edge), jnp.bfloat16),
            pltpu.VMEM((SPREAD, width, edge), jnp.float32),
            pltpu.SemaphoreType.DMA((slots,)),
        ],
        cost_estimate=cost,
        name="backward",
    )(rows, cols, count, tiles, slab_grads)
    terms = [
        term if offset == REACH else shifted(term, "dom", offset - REACH)
        for offset, term in enumerate(terms)
    ]
    grad_features = pl.pallas_call(
        features_kernel,
        out_shape=block,
        in_specs=[VMEM] * (SPREAD + 1),
        out_specs=VMEM,
        name="features",
    )(*terms, weight)
    projected = pl.pallas_call(
        project_kernel,
        out_shape=block,
        in_specs=[VMEM] * 2,
        out_specs=VMEM,
        name="project",
    )(slab_parts, weight)
    return projected, grad_features


def solution(mesh):
    placed = (
        P(("dom", "repl"), None),
        P(),
        P(("dom", "repl"), None),
        P("dom", "repl", None, None, None),
        P("dom", "repl", None),
        P("dom", "repl", None),
        P("dom", "repl"),
    )
    return jax.shard_map(
        body,
        mesh=mesh,
        in_specs=placed,
        out_specs=(P(("dom", "repl"), None), P(("dom", "repl"), None)),
        check_vma=False,
    )
```

```python
import jax
import jax.numpy as jnp
from jax import lax
from jax.experimental import pallas as pl
from jax.experimental.pallas import tpu as pltpu
from jax.sharding import PartitionSpec as P

REACH = 2
SPREAD = 2 * REACH + 1
TOGETHER = 2
LIMIT = pltpu.CompilerParams(vmem_limit_bytes=16 * 2**20)

SMEM = pl.BlockSpec(memory_space=pltpu.SMEM)
VMEM = pl.BlockSpec(memory_space=pltpu.VMEM)
ANY = pl.BlockSpec(memory_space=pl.ANY)
HBM = pl.BlockSpec(memory_space=pltpu.HBM)


def in_hbm(array):
    return pltpu.with_memory_space_constraint(array, pltpu.HBM)


def shifted(array, axis, by):
    devices = lax.axis_size(axis)
    pairs = [(i, i + by) for i in range(devices) if 0 <= i + by < devices]
    return lax.ppermute(array, axis, pairs)


def spread_kernel(grads, spread, block, turned, load_sem, sems):
    load = pltpu.make_async_copy(grads, block, load_sem)
    load.start()
    load.wait()
    turned[...] = block[...].T
    copies = [
        pltpu.make_async_copy(turned, spread.at[index], sems.at[index])
        for index in range(spread.shape[0])
    ]
    for copy in copies:
        copy.start()
    for copy in copies:
        copy.wait()


def split_slots(cols, live, lists):
    def place(slot, lengths):
        even, odd = lengths
        is_odd = lax.rem(cols[slot], 2)
        lists[is_odd, jnp.where(is_odd == 1, odd, even)] = slot
        return even + 1 - is_odd, odd + is_odd

    zero = jnp.int32(0)
    return lax.fori_loop(0, live, place, (zero, zero))


def early_kernel(
    rows_from, cols_from, count_from, tiles, features, grads, below, above,
    held, up, down, ends,
    rows, cols, count, lists, back, ready, int_sems, tile_sems, block_sems, send_sems,
):
    def fetch(slot):
        return pltpu.make_async_copy(tiles.at[slot], held.at[slot], tile_sems.at[slot])

    ints = [
        pltpu.make_async_copy(source, target, int_sems.at[index])
        for index, (source, target) in enumerate(
            ((count_from, count), (rows_from, rows), (cols_from, cols))
        )
    ]
    for copy in ints:
        copy.start()
    own = [pltpu.make_async_copy(features, ends.at[1], block_sems.at[0])]
    own[0].start()
    back[...] = jnp.zeros_like(back)
    ends[0] = below[...]
    ends[2] = above[...]
    ints[0].wait()
    live = count[0]

    @pl.loop(0, live)
    def _(slot):
        fetch(slot).start()

    ints[1].wait()
    ints[2].wait()
    own[0].wait()
    own = [
        pltpu.make_async_copy(ends.at[1], target.at[1], block_sems.at[1 + index])
        for index, target in enumerate((up, down))
    ]
    for copy in own:
        copy.start()
    even, odd = split_slots(cols, live, lists)

    @pl.loop(0, lax.div(odd + TOGETHER - 1, TOGETHER))
    def _(step):
        sums = []
        slots = []
        for k in range(TOGETHER):
            place = step * TOGETHER + k
            slot = lists[1, jnp.minimum(place, odd - 1)]
            slots.append((place < odd, slot))

            @pl.when(place < odd)
            def _():
                fetch(slot).wait()

        for used, slot in slots:
            term = jnp.dot(grads[rows[slot]], held[slot], preferred_element_type=jnp.float32)
            sums.append((jnp.where(used, lax.div(cols[slot], 2), 2), term))
        for index, term in sums:
            back[index] += term

    sends = []
    for index, target in enumerate((down, up)):
        ready[index] = back[index].T.astype(ready.dtype)
        sends.append(pltpu.make_async_copy(ready.at[index], target.at[0], send_sems.at[index]))
        sends[-1].start()

    @pl.loop(0, even)
    def _(place):
        fetch(lists[0, place]).wait()

    for copy in sends + own:
        copy.wait()


def late_kernel(
    rows_from, cols_from, count_from, held, grads, ends, from_below, from_above,
    parts, far_down, far_up, kept,
    rows, cols, count, lists, near, total, back, staged, ready, sums_here, int_sems, send_sems,
):
    blocks = grads.shape[0]
    ints = [
        pltpu.make_async_copy(source, target, int_sems.at[index])
        for index, (source, target) in enumerate(
            ((count_from, count), (rows_from, rows), (cols_from, cols))
        )
    ]
    for copy in ints:
        copy.start()
    near[0] = ends[0]
    near[1] = from_below[1]
    near[2] = ends[1]
    near[3] = from_above[1]
    near[4] = ends[2]
    total[...] = jnp.zeros_like(total)
    back[...] = jnp.zeros_like(back)
    for copy in ints:
        copy.wait()
    even, odd = split_slots(cols, count[0], lists)

    def run(parity, length):
        @pl.loop(0, lax.div(length + TOGETHER - 1, TOGETHER))
        def _(step):
            sums = []
            for k in range(TOGETHER):
                place = step * TOGETHER + k
                slot = lists[parity, jnp.minimum(place, length - 1)]
                used = place < length
                row, col = rows[slot], cols[slot]
                tile = held[slot]
                ahead = jnp.dot(tile, near[col], preferred_element_type=jnp.float32)
                sums.append((total, jnp.where(used, row, blocks), ahead))
                if parity == 0:
                    behind = jnp.dot(grads[row], tile, preferred_element_type=jnp.float32)
                    sums.append((back, jnp.where(used, lax.div(col, 2), 3), behind))
            for target, index, term in sums:
                target[index] += term

    run(0, even)
    run(1, odd)

    copies = []
    for block in range(blocks):
        staged[block] = total[block].astype(staged.dtype)
        copies.append(
            pltpu.make_async_copy(staged.at[block], parts.at[block], send_sems.at[block])
        )
        copies[-1].start()
    for index, target in enumerate((far_down, far_up)):
        ready[index] = back[2 * index].astype(ready.dtype)
        copies.append(
            pltpu.make_async_copy(ready.at[index], target, send_sems.at[blocks + index])
        )
        copies[-1].start()
    sums_here[...] = (
        back[1].T + from_below[0].astype(jnp.float32) + from_above[0].astype(jnp.float32)
    )
    copies.append(pltpu.make_async_copy(sums_here, kept, send_sems.at[blocks + 2]))
    copies[-1].start()
    for copy in copies:
        copy.wait()


def project_kernel(parts, weight, kept, out, kept_out):
    total = jnp.sum(parts[...].astype(jnp.float32), axis=0)
    out[...] = jnp.dot(
        total.astype(jnp.bfloat16), weight[...], preferred_element_type=jnp.float32
    ).astype(out.dtype)
    kept_out[...] = kept[...]


def features_kernel(kept, from_below, from_above, weight, out):
    far = from_below[...].astype(jnp.float32) + from_above[...].astype(jnp.float32)
    total = kept[...] + far.T
    out[...] = lax.dot_general(
        total.astype(jnp.bfloat16),
        weight[...],
        (((1,), (1,)), ((), ())),
        preferred_element_type=jnp.float32,
    ).astype(out.dtype)


def body(features, weight, grad_out, tile_values, tile_rows, tile_cols, tile_count):
    slots, edge = tile_values.shape[2], tile_values.shape[3]
    width = features.shape[1]
    blocks = lax.axis_size("repl")
    tiles = in_hbm(tile_values.reshape(slots, edge, edge))
    ints = [
        in_hbm(tile_rows.reshape(slots)),
        in_hbm(tile_cols.reshape(slots)),
        tile_count.reshape(1),
    ]
    int_scratch = [
        pltpu.SMEM((slots,), jnp.int32),
        pltpu.SMEM((slots,), jnp.int32),
        pltpu.SMEM((1,), jnp.int32),
        pltpu.SMEM((2, slots), jnp.int32),
    ]
    flops = 2 * slots * edge * edge * width
    moved = slots * edge * edge * 2

    spread = pl.pallas_call(
        spread_kernel,
        out_shape=pltpu.HBM((blocks, width, edge), jnp.bfloat16),
        in_specs=[HBM],
        out_specs=HBM,
        scratch_shapes=[
            pltpu.VMEM((edge, width), jnp.bfloat16),
            pltpu.VMEM((width, edge), jnp.bfloat16),
            pltpu.SemaphoreType.DMA,
            pltpu.SemaphoreType.DMA((blocks,)),
        ],
        compiler_params=LIMIT,
        name="spread",
    )(in_hbm(grad_out))
    slab_grads = lax.all_to_all(spread, "repl", 0, 0, tiled=True)
    below = shifted(features, "dom", REACH)
    above = shifted(features, "dom", -REACH)
    held, up, down, ends = pl.pallas_call(
        early_kernel,
        out_shape=[
            pltpu.VMEM((slots, edge, edge), jnp.bfloat16),
            pltpu.HBM((2, edge, width), jnp.bfloat16),
            pltpu.HBM((2, edge, width), jnp.bfloat16),
            pltpu.VMEM((3, edge, width), jnp.bfloat16),
        ],
        in_specs=[HBM] * 2 + [ANY] + [HBM] * 2 + [VMEM] * 3,
        out_specs=[VMEM, HBM, HBM, VMEM],
        scratch_shapes=int_scratch
        + [
            pltpu.VMEM((3, width, edge), jnp.float32),
            pltpu.VMEM((2, edge, width), jnp.bfloat16),
            pltpu.SemaphoreType.DMA((3,)),
            pltpu.SemaphoreType.DMA((slots,)),
            pltpu.SemaphoreType.DMA((3,)),
            pltpu.SemaphoreType.DMA((2,)),
        ],
        cost_estimate=pl.CostEstimate(flops=flops, bytes_accessed=moved, transcendentals=0),
        compiler_params=LIMIT,
        name="early",
    )(*ints, tiles, in_hbm(features), slab_grads, below, above)
    from_below = shifted(up, "dom", 1)
    from_above = shifted(down, "dom", -1)
    partial, far_down, far_up, kept = pl.pallas_call(
        late_kernel,
        out_shape=[
            pltpu.HBM((blocks, edge, width), jnp.bfloat16),
            pltpu.HBM((width, edge), jnp.bfloat16),
            pltpu.HBM((width, edge), jnp.bfloat16),
            pltpu.HBM((edge, width), jnp.float32),
        ],
        in_specs=[HBM] * 2 + [ANY] + [VMEM] * 5,
        out_specs=[HBM] * 4,
        scratch_shapes=int_scratch
        + [
            pltpu.VMEM((SPREAD, edge, width), jnp.bfloat16),
            pltpu.VMEM((blocks + 1, edge, width), jnp.float32),
            pltpu.VMEM((4, width, edge), jnp.float32),
            pltpu.VMEM((blocks, edge, width), jnp.bfloat16),
            pltpu.VMEM((2, width, edge), jnp.bfloat16),
            pltpu.VMEM((edge, width), jnp.float32),
            pltpu.SemaphoreType.DMA((3,)),
            pltpu.SemaphoreType.DMA((blocks + 3,)),
        ],
        cost_estimate=pl.CostEstimate(flops=flops, bytes_accessed=moved, transcendentals=0),
        compiler_params=LIMIT,
        name="late",
    )(*ints, held, slab_grads, ends, from_below, from_above)
    slab_parts = lax.all_to_all(partial, "repl", 0, 0, tiled=True)
    far_from_above = shifted(far_down, "dom", -REACH)
    far_from_below = shifted(far_up, "dom", REACH)
    projected, kept = pl.pallas_call(
        project_kernel,
        out_shape=[
            jax.ShapeDtypeStruct((edge, width), jnp.bfloat16),
            pltpu.VMEM((edge, width), jnp.float32),
        ],
        in_specs=[VMEM] * 3,
        out_specs=[VMEM] * 2,
        compiler_params=LIMIT,
        name="project",
    )(slab_parts, weight, in_hbm(kept))
    grad_features = pl.pallas_call(
        features_kernel,
        out_shape=jax.ShapeDtypeStruct((edge, width), jnp.bfloat16),
        in_specs=[VMEM] * 4,
        out_specs=VMEM,
        compiler_params=LIMIT,
        name="features",
    )(kept, far_from_below, far_from_above, weight)
    return projected, grad_features


def solution(mesh):
    placed = (
        P(("dom", "repl"), None),
        P(),
        P(("dom", "repl"), None),
        P("dom", "repl", None, None, None),
        P("dom", "repl", None),
        P("dom", "repl", None),
        P("dom", "repl"),
    )
    return jax.shard_map(
        body,
        mesh=mesh,
        in_specs=placed,
        out_specs=(P(("dom", "repl"), None), P(("dom", "repl"), None)),
        check_vma=False,
    )
```

```python
import jax
import jax.numpy as jnp
from jax import lax
from jax.experimental import pallas as pl
from jax.experimental.pallas import tpu as pltpu
from jax.sharding import PartitionSpec as P

REACH = 2
SPREAD = 2 * REACH + 1
TOGETHER = 4
LIMIT = pltpu.CompilerParams(vmem_limit_bytes=16 * 2**20)

SMEM = pl.BlockSpec(memory_space=pltpu.SMEM)
VMEM = pl.BlockSpec(memory_space=pltpu.VMEM)
ANY = pl.BlockSpec(memory_space=pl.ANY)
HBM = pl.BlockSpec(memory_space=pltpu.HBM)


def in_hbm(array):
    return pltpu.with_memory_space_constraint(array, pltpu.HBM)


def shifted(array, axis, by):
    devices = lax.axis_size(axis)
    pairs = [(i, i + by) for i in range(devices) if 0 <= i + by < devices]
    return lax.ppermute(array, axis, pairs)


def spread_kernel(grads, spread, block, load_sem):
    load = pltpu.make_async_copy(grads, block, load_sem)
    load.start()
    load.wait()
    turned = block[...].T
    for index in range(spread.shape[0]):
        spread[index] = turned


def split_slots(cols, live, lists):
    def place(slot, lengths):
        even, odd = lengths
        is_odd = lax.rem(cols[slot], 2)
        lists[is_odd, jnp.where(is_odd == 1, odd, even)] = slot
        return even + 1 - is_odd, odd + is_odd

    zero = jnp.int32(0)
    return lax.fori_loop(0, live, place, (zero, zero))


def early_kernel(
    rows_from, cols_from, count_from, tiles, features, grads, below, above,
    held, up, down, ends,
    rows, cols, count, lists, back, int_sems, tile_sems, own_sems,
):
    def fetch(slot):
        return pltpu.make_async_copy(tiles.at[slot], held.at[slot], tile_sems.at[slot])

    ints = [
        pltpu.make_async_copy(source, target, int_sems.at[index])
        for index, (source, target) in enumerate(
            ((count_from, count), (rows_from, rows), (cols_from, cols))
        )
    ]
    for copy in ints:
        copy.start()
    own = [
        pltpu.make_async_copy(features, target, own_sems.at[index])
        for index, target in enumerate((ends.at[1], up.at[1], down.at[1]))
    ]
    for copy in own:
        copy.start()
    for slot in range(held.shape[0]):
        fetch(slot).start()
    back[...] = jnp.zeros_like(back)
    ends[0] = below[...]
    ends[2] = above[...]
    for copy in ints:
        copy.wait()
    even, odd = split_slots(cols, count[0], lists)

    @pl.loop(0, lax.div(odd + TOGETHER - 1, TOGETHER))
    def _(step):
        sums = []
        slots = []
        for k in range(TOGETHER):
            place = step * TOGETHER + k
            slot = lists[1, jnp.minimum(place, odd - 1)]
            slots.append((place < odd, slot))

            @pl.when(place < odd)
            def _():
                fetch(slot).wait()

        for used, slot in slots:
            term = jnp.dot(grads[rows[slot]], held[slot], preferred_element_type=jnp.float32)
            sums.append((jnp.where(used, lax.div(cols[slot], 2), 2), term))
        for index, term in sums:
            back[index] += term

    for index, target in enumerate((down, up)):
        target[0] = back[index].T.astype(target.dtype)

    @pl.loop(0, even)
    def _(place):
        fetch(lists[0, place]).wait()

    @pl.loop(count[0], held.shape[0])
    def _(slot):
        fetch(slot).wait()

    for copy in own:
        copy.wait()


def load_ints(rows_from, cols_from, count_from, rows, cols, count, sems):
    copies = [
        pltpu.make_async_copy(source, target, sems.at[index])
        for index, (source, target) in enumerate(
            ((count_from, count), (rows_from, rows), (cols_from, cols))
        )
    ]
    for copy in copies:
        copy.start()
    return copies


def middle_kernel(
    rows_from, cols_from, count_from, held, grads, ends,
    sums, far_down, center, far_up,
    rows, cols, count, lists, total, back, int_sems,
):
    blocks = grads.shape[0]
    ints = load_ints(rows_from, cols_from, count_from, rows, cols, count, int_sems)
    total[...] = jnp.zeros_like(total)
    back[...] = jnp.zeros_like(back)
    for copy in ints:
        copy.wait()
    even, _ = split_slots(cols, count[0], lists)

    @pl.loop(0, lax.div(even + TOGETHER - 1, TOGETHER))
    def _(step):
        terms = []
        for k in range(TOGETHER):
            place = step * TOGETHER + k
            slot = lists[0, jnp.minimum(place, even - 1)]
            used = place < even
            row, side = rows[slot], lax.div(cols[slot], 2)
            tile = held[slot]
            ahead = jnp.dot(tile, ends[side], preferred_element_type=jnp.float32)
            behind = jnp.dot(grads[row], tile, preferred_element_type=jnp.float32)
            terms.append((total, jnp.where(used, row, blocks), ahead))
            terms.append((back, jnp.where(used, side, 3), behind))
        for target, index, term in terms:
            target[index] += term

    sums[...] = total[pl.ds(0, blocks)]
    for side, ref in enumerate((far_down, center, far_up)):
        ref[...] = back[side].astype(ref.dtype)


def late_kernel(
    rows_from, cols_from, count_from, held, sums, center, from_below, from_above,
    parts, kept,
    rows, cols, count, lists, near, total, int_sems,
):
    blocks = sums.shape[0]
    ints = load_ints(rows_from, cols_from, count_from, rows, cols, count, int_sems)
    near[0] = from_below[1]
    near[1] = from_above[1]
    total[pl.ds(0, blocks)] = sums[...]
    for copy in ints:
        copy.wait()
    _, odd = split_slots(cols, count[0], lists)

    @pl.loop(0, lax.div(odd + TOGETHER - 1, TOGETHER))
    def _(step):
        terms = []
        for k in range(TOGETHER):
            place = step * TOGETHER + k
            slot = lists[1, jnp.minimum(place, odd - 1)]
            ahead = jnp.dot(
                held[slot], near[lax.div(cols[slot], 2)], preferred_element_type=jnp.float32
            )
            terms.append((jnp.where(place < odd, rows[slot], blocks), ahead))
        for index, term in terms:
            total[index] += term

    parts[...] = total[pl.ds(0, blocks)].astype(parts.dtype)
    kept[...] = (
        center[...].T + from_below[0].astype(jnp.float32) + from_above[0].astype(jnp.float32)
    )


def project_kernel(parts, weight, kept, out, kept_out):
    total = jnp.sum(parts[...].astype(jnp.float32), axis=0)
    out[...] = jnp.dot(
        total.astype(jnp.bfloat16), weight[...], preferred_element_type=jnp.float32
    ).astype(out.dtype)
    kept_out[...] = kept[...]


def features_kernel(kept, from_below, from_above, weight, out):
    far = from_below[...].astype(jnp.float32) + from_above[...].astype(jnp.float32)
    total = kept[...] + far.T
    out[...] = lax.dot_general(
        total.astype(jnp.bfloat16),
        weight[...],
        (((1,), (1,)), ((), ())),
        preferred_element_type=jnp.float32,
    ).astype(out.dtype)


def body(features, weight, grad_out, tile_values, tile_rows, tile_cols, tile_count):
    slots, edge = tile_values.shape[2], tile_values.shape[3]
    width = features.shape[1]
    blocks = lax.axis_size("repl")
    tiles = in_hbm(tile_values.reshape(slots, edge, edge))
    ints = [
        in_hbm(tile_rows.reshape(slots)),
        in_hbm(tile_cols.reshape(slots)),
        tile_count.reshape(1),
    ]
    int_scratch = [
        pltpu.SMEM((slots,), jnp.int32),
        pltpu.SMEM((slots,), jnp.int32),
        pltpu.SMEM((1,), jnp.int32),
        pltpu.SMEM((2, slots), jnp.int32),
    ]
    flops = 2 * slots * edge * edge * width
    moved = slots * edge * edge * 2

    spread = pl.pallas_call(
        spread_kernel,
        out_shape=pltpu.VMEM((blocks, width, edge), jnp.bfloat16),
        in_specs=[HBM],
        out_specs=VMEM,
        scratch_shapes=[
            pltpu.VMEM((edge, width), jnp.bfloat16),
            pltpu.SemaphoreType.DMA,
        ],
        compiler_params=LIMIT,
        name="spread",
    )(in_hbm(grad_out))
    slab_grads = lax.all_to_all(spread, "repl", 0, 0, tiled=True)
    below = shifted(features, "dom", REACH)
    above = shifted(features, "dom", -REACH)
    held, up, down, ends = pl.pallas_call(
        early_kernel,
        out_shape=[
            pltpu.VMEM((slots, edge, edge), jnp.bfloat16),
            pltpu.VMEM((2, edge, width), jnp.bfloat16),
            pltpu.VMEM((2, edge, width), jnp.bfloat16),
            pltpu.VMEM((3, edge, width), jnp.bfloat16),
        ],
        in_specs=[HBM] * 2 + [ANY] + [HBM] * 2 + [VMEM] * 3,
        out_specs=[VMEM] * 4,
        scratch_shapes=int_scratch
        + [
            pltpu.VMEM((3, width, edge), jnp.float32),
            pltpu.SemaphoreType.DMA((3,)),
            pltpu.SemaphoreType.DMA((slots,)),
            pltpu.SemaphoreType.DMA((3,)),
        ],
        cost_estimate=pl.CostEstimate(flops=flops, bytes_accessed=moved, transcendentals=0),
        compiler_params=LIMIT,
        name="early",
    )(*ints, tiles, in_hbm(features), slab_grads, below, above)
    from_below = shifted(up, "dom", 1)
    from_above = shifted(down, "dom", -1)
    cost = pl.CostEstimate(flops=flops, bytes_accessed=moved, transcendentals=0)
    term = pltpu.VMEM((width, edge), jnp.bfloat16)
    sums, far_down, center, far_up = pl.pallas_call(
        middle_kernel,
        out_shape=[
            pltpu.VMEM((blocks, edge, width), jnp.float32),
            term,
            pltpu.VMEM((width, edge), jnp.float32),
            term,
        ],
        in_specs=[HBM] * 2 + [ANY] + [VMEM] * 3,
        out_specs=[VMEM] * 4,
        scratch_shapes=int_scratch
        + [
            pltpu.VMEM((blocks + 1, edge, width), jnp.float32),
            pltpu.VMEM((4, width, edge), jnp.float32),
            pltpu.SemaphoreType.DMA((3,)),
        ],
        cost_estimate=cost,
        compiler_params=LIMIT,
        name="middle",
    )(*ints, held, slab_grads, ends)
    partial, kept = pl.pallas_call(
        late_kernel,
        out_shape=[
            pltpu.VMEM((blocks, edge, width), jnp.bfloat16),
            pltpu.VMEM((edge, width), jnp.float32),
        ],
        in_specs=[HBM] * 2 + [ANY] + [VMEM] * 5,
        out_specs=[VMEM] * 2,
        scratch_shapes=int_scratch
        + [
            pltpu.VMEM((2, edge, width), jnp.bfloat16),
            pltpu.VMEM((blocks + 1, edge, width), jnp.float32),
            pltpu.SemaphoreType.DMA((3,)),
        ],
        cost_estimate=cost,
        compiler_params=LIMIT,
        name="late",
    )(*ints, held, sums, center, from_below, from_above)
    slab_parts = lax.all_to_all(partial, "repl", 0, 0, tiled=True)
    far_from_above = shifted(far_down, "dom", -REACH)
    far_from_below = shifted(far_up, "dom", REACH)
    block = jax.ShapeDtypeStruct((edge, width), jnp.bfloat16)
    projected, kept = pl.pallas_call(
        project_kernel,
        out_shape=[block, pltpu.VMEM((edge, width), jnp.float32)],
        in_specs=[VMEM] * 3,
        out_specs=[VMEM] * 2,
        compiler_params=LIMIT,
        name="project",
    )(slab_parts, weight, kept)
    grad_features = pl.pallas_call(
        features_kernel,
        out_shape=block,
        in_specs=[VMEM] * 4,
        out_specs=VMEM,
        compiler_params=LIMIT,
        name="features",
    )(kept, far_from_below, far_from_above, weight)
    return projected, grad_features


def solution(mesh):
    placed = (
        P(("dom", "repl"), None),
        P(),
        P(("dom", "repl"), None),
        P("dom", "repl", None, None, None),
        P("dom", "repl", None),
        P("dom", "repl", None),
        P("dom", "repl"),
    )
    return jax.shard_map(
        body,
        mesh=mesh,
        in_specs=placed,
        out_specs=(P(("dom", "repl"), None), P(("dom", "repl"), None)),
        check_vma=False,
    )
```

```python
import jax
import jax.numpy as jnp
from jax import lax
from jax.experimental import pallas as pl
from jax.experimental.pallas import tpu as pltpu
from jax.sharding import PartitionSpec as P

REACH = 2
SPREAD = 2 * REACH + 1
TOGETHER = 4
KEPT = 22
LIMIT = pltpu.CompilerParams(vmem_limit_bytes=16 * 2**20)

SMEM = pl.BlockSpec(memory_space=pltpu.SMEM)
VMEM = pl.BlockSpec(memory_space=pltpu.VMEM)
ANY = pl.BlockSpec(memory_space=pl.ANY)
HBM = pl.BlockSpec(memory_space=pltpu.HBM)


def in_hbm(array):
    return pltpu.with_memory_space_constraint(array, pltpu.HBM)


def shifted(array, axis, by):
    devices = lax.axis_size(axis)
    pairs = [(i, i + by) for i in range(devices) if 0 <= i + by < devices]
    return lax.ppermute(array, axis, pairs)


def spread_kernel(
    grads, rows_from, cols_from, spread, rows, cols, block, sems
):
    loads = [
        pltpu.make_async_copy(source, target, sems.at[index])
        for index, (source, target) in enumerate(
            ((grads, block), (rows_from, rows), (cols_from, cols))
        )
    ]
    for load in loads:
        load.start()
    loads[0].wait()
    turned = block[...].T
    for index in range(spread.shape[0]):
        spread[index] = turned
    for load in loads[1:]:
        load.wait()


def split_slots(cols, live, lists):
    def place(slot, lengths):
        even, odd = lengths
        is_odd = lax.rem(cols[slot], 2)
        lists[is_odd, jnp.where(is_odd == 1, odd, even)] = slot
        return even + 1 - is_odd, odd + is_odd

    zero = jnp.int32(0)
    return lax.fori_loop(0, live, place, (zero, zero))


def hold_kernel(cols, count, tiles, held, lists, sems):
    _, odd = split_slots(cols, count[0, 0], lists)

    def fetch(place):
        return pltpu.make_async_copy(tiles.at[lists[1, place]], held.at[place], sems.at[place])

    @pl.loop(0, jnp.minimum(odd, KEPT))
    def _(place):
        fetch(place).start()

    @pl.loop(0, jnp.minimum(odd, KEPT))
    def _(place):
        fetch(place).wait()


def over_odd_tiles(lists, odd, tiles, held, extra, extra_sem, product, add):
    ready = jnp.minimum(odd, KEPT)

    @pl.loop(0, lax.div(ready + TOGETHER - 1, TOGETHER))
    def _(step):
        terms = []
        for k in range(TOGETHER):
            place = step * TOGETHER + k
            inside = jnp.minimum(place, ready - 1)
            slot = lists[1, inside]
            terms.append((slot, place < ready, product(slot, held[inside])))
        for slot, used, term in terms:
            add(slot, used, term)

    @pl.loop(ready, odd)
    def _(place):
        slot = lists[1, place]
        copy = pltpu.make_async_copy(tiles.at[slot], extra, extra_sem)
        copy.start()
        copy.wait()
        add(slot, True, product(slot, extra[...]))


def early_kernel(
    rows, cols, count, tiles, features, held, grads, below, above,
    up, down, ends,
    lists, back, extra, extra_sem, own_sems,
):
    own = [
        pltpu.make_async_copy(features, target, own_sems.at[index])
        for index, target in enumerate((ends.at[1], up.at[1], down.at[1]))
    ]
    for copy in own:
        copy.start()
    back[...] = jnp.zeros_like(back)
    ends[0] = below[...]
    ends[2] = above[...]
    _, odd = split_slots(cols, count[0, 0], lists)

    def product(slot, tile):
        return jnp.dot(grads[rows[slot]], tile, preferred_element_type=jnp.float32)

    def add(slot, used, term):
        back[jnp.where(used, lax.div(cols[slot], 2), 2)] += term

    over_odd_tiles(lists, odd, tiles, held, extra, extra_sem, product, add)
    for index, target in enumerate((down, up)):
        target[0] = back[index].T.astype(target.dtype)
    for copy in own:
        copy.wait()


def middle_kernel(
    rows, cols, count, tiles, grads, ends,
    sums, far_down, center, far_up,
    lists, held, total, back, sems,
):
    blocks = grads.shape[0]
    even, _ = split_slots(cols, count[0, 0], lists)

    def fetch(place):
        return pltpu.make_async_copy(tiles.at[lists[0, place]], held.at[place], sems.at[place])

    @pl.loop(0, even)
    def _(place):
        fetch(place).start()

    total[...] = jnp.zeros_like(total)
    back[...] = jnp.zeros_like(back)

    @pl.loop(0, lax.div(even + TOGETHER - 1, TOGETHER))
    def _(step):
        terms = []
        for k in range(TOGETHER):
            place = step * TOGETHER + k

            @pl.when(place < even)
            def _():
                fetch(place).wait()

        for k in range(TOGETHER):
            place = step * TOGETHER + k
            inside = jnp.minimum(place, even - 1)
            slot = lists[0, inside]
            used = place < even
            row, side = rows[slot], lax.div(cols[slot], 2)
            tile = held[inside]
            ahead = jnp.dot(tile, ends[side], preferred_element_type=jnp.float32)
            behind = jnp.dot(grads[row], tile, preferred_element_type=jnp.float32)
            terms.append((total, jnp.where(used, row, blocks), ahead))
            terms.append((back, jnp.where(used, side, 3), behind))
        for target, index, term in terms:
            target[index] += term

    sums[...] = total[pl.ds(0, blocks)]
    for side, ref in enumerate((far_down, center, far_up)):
        ref[...] = back[side].astype(ref.dtype)


def late_kernel(
    rows, cols, count, tiles, held, sums, center, from_above, from_below,
    parts, kept,
    lists, near, total, extra, extra_sem,
):
    blocks = sums.shape[0]
    near[0] = from_below[1]
    near[1] = from_above[1]
    total[pl.ds(0, blocks)] = sums[...]
    _, odd = split_slots(cols, count[0, 0], lists)

    def product(slot, tile):
        block = near[lax.div(cols[slot], 2)]
        return jnp.dot(tile, block, preferred_element_type=jnp.float32)

    def add(slot, used, term):
        total[jnp.where(used, rows[slot], blocks)] += term

    over_odd_tiles(lists, odd, tiles, held, extra, extra_sem, product, add)
    parts[...] = total[pl.ds(0, blocks)].astype(parts.dtype)
    kept[...] = (
        center[...].T + from_below[0].astype(jnp.float32) + from_above[0].astype(jnp.float32)
    )


def project_kernel(parts, weight, kept, out, kept_out):
    total = jnp.sum(parts[...].astype(jnp.float32), axis=0)
    out[...] = jnp.dot(
        total.astype(jnp.bfloat16), weight[...], preferred_element_type=jnp.float32
    ).astype(out.dtype)
    kept_out[...] = kept[...]


def features_kernel(kept, from_below, from_above, weight, out):
    far = from_below[...].astype(jnp.float32) + from_above[...].astype(jnp.float32)
    total = kept[...] + far.T
    out[...] = lax.dot_general(
        total.astype(jnp.bfloat16),
        weight[...],
        (((1,), (1,)), ((), ())),
        preferred_element_type=jnp.float32,
    ).astype(out.dtype)


def body(features, weight, grad_out, tile_values, tile_rows, tile_cols, tile_count):
    slots, edge = tile_values.shape[2], tile_values.shape[3]
    width = features.shape[1]
    blocks = lax.axis_size("repl")
    tiles = in_hbm(tile_values.reshape(slots, edge, edge))
    ints = [
        in_hbm(tile_rows.reshape(slots)),
        in_hbm(tile_cols.reshape(slots)),
    ]
    flops = 2 * slots * edge * edge * width
    moved = slots * edge * edge * 2

    spread, *ints = pl.pallas_call(
        spread_kernel,
        out_shape=[
            pltpu.VMEM((blocks, width, edge), jnp.bfloat16),
            pltpu.VMEM((slots,), jnp.int32),
            pltpu.VMEM((slots,), jnp.int32),
        ],
        in_specs=[HBM] * 3,
        out_specs=[VMEM] * 3,
        scratch_shapes=[
            pltpu.VMEM((edge, width), jnp.bfloat16),
            pltpu.SemaphoreType.DMA((3,)),
        ],
        compiler_params=LIMIT,
        name="spread",
    )(in_hbm(grad_out), *ints)
    slab_grads = lax.all_to_all(spread, "repl", 0, 0, tiled=True)
    below = shifted(features, "dom", REACH)
    above = shifted(features, "dom", -REACH)
    lists = pltpu.SMEM((2, slots), jnp.int32)
    extra = [pltpu.VMEM((edge, edge), jnp.bfloat16), pltpu.SemaphoreType.DMA]
    held = pl.pallas_call(
        hold_kernel,
        out_shape=pltpu.VMEM((KEPT, edge, edge), jnp.bfloat16),
        in_specs=[SMEM] * 2 + [HBM],
        out_specs=VMEM,
        scratch_shapes=[lists, pltpu.SemaphoreType.DMA((KEPT,))],
        cost_estimate=pl.CostEstimate(flops=0, bytes_accessed=moved, transcendentals=0),
        compiler_params=LIMIT,
        name="hold",
    )(ints[1], tile_count, tiles)
    packed = pltpu.VMEM((2, edge, width), jnp.bfloat16)
    up, down, ends = pl.pallas_call(
        early_kernel,
        out_shape=[packed, packed, pltpu.VMEM((3, edge, width), jnp.bfloat16)],
        in_specs=[SMEM] * 3 + [HBM] * 2 + [VMEM] * 4,
        out_specs=[VMEM] * 3,
        scratch_shapes=[lists, pltpu.VMEM((3, width, edge), jnp.float32)]
        + extra
        + [pltpu.SemaphoreType.DMA((3,))],
        cost_estimate=pl.CostEstimate(flops=flops, bytes_accessed=moved, transcendentals=0),
        compiler_params=LIMIT,
        name="early",
    )(*ints, tile_count, tiles, in_hbm(features), held, slab_grads, below, above)
    from_above = shifted(down, "dom", -1)
    from_below = shifted(up, "dom", 1)
    cost = pl.CostEstimate(flops=flops, bytes_accessed=moved, transcendentals=0)
    term = pltpu.VMEM((width, edge), jnp.bfloat16)
    sums, far_down, center, far_up = pl.pallas_call(
        middle_kernel,
        out_shape=[
            pltpu.VMEM((blocks, edge, width), jnp.float32),
            term,
            pltpu.VMEM((width, edge), jnp.float32),
            term,
        ],
        in_specs=[SMEM] * 3 + [HBM] + [VMEM] * 2,
        out_specs=[VMEM] * 4,
        scratch_shapes=[
            lists,
            pltpu.VMEM((slots, edge, edge), jnp.bfloat16),
            pltpu.VMEM((blocks + 1, edge, width), jnp.float32),
            pltpu.VMEM((4, width, edge), jnp.float32),
            pltpu.SemaphoreType.DMA((slots,)),
        ],
        cost_estimate=cost,
        compiler_params=LIMIT,
        name="middle",
    )(*ints, tile_count, tiles, slab_grads, ends)
    partial, kept = pl.pallas_call(
        late_kernel,
        out_shape=[
            pltpu.VMEM((blocks, edge, width), jnp.bfloat16),
            pltpu.VMEM((edge, width), jnp.float32),
        ],
        in_specs=[SMEM] * 3 + [HBM] + [VMEM] * 5,
        out_specs=[VMEM] * 2,
        scratch_shapes=[
            lists,
            pltpu.VMEM((2, edge, width), jnp.bfloat16),
            pltpu.VMEM((blocks + 1, edge, width), jnp.float32),
        ]
        + extra,
        cost_estimate=cost,
        compiler_params=LIMIT,
        name="late",
    )(*ints, tile_count, tiles, held, sums, center, from_above, from_below)
    slab_parts = lax.all_to_all(partial, "repl", 0, 0, tiled=True)
    far_from_above = shifted(far_down, "dom", -REACH)
    far_from_below = shifted(far_up, "dom", REACH)
    block = jax.ShapeDtypeStruct((edge, width), jnp.bfloat16)
    projected, kept = pl.pallas_call(
        project_kernel,
        out_shape=[block, pltpu.VMEM((edge, width), jnp.float32)],
        in_specs=[VMEM] * 3,
        out_specs=[VMEM] * 2,
        compiler_params=LIMIT,
        name="project",
    )(slab_parts, weight, kept)
    grad_features = pl.pallas_call(
        features_kernel,
        out_shape=block,
        in_specs=[VMEM] * 4,
        out_specs=VMEM,
        compiler_params=LIMIT,
        name="features",
    )(kept, far_from_above, far_from_below, weight)
    return projected, grad_features


def solution(mesh):
    placed = (
        P(("dom", "repl"), None),
        P(),
        P(("dom", "repl"), None),
        P("dom", "repl", None, None, None),
        P("dom", "repl", None),
        P("dom", "repl", None),
        P("dom", "repl"),
    )
    return jax.shard_map(
        body,
        mesh=mesh,
        in_specs=placed,
        out_specs=(P(("dom", "repl"), None), P(("dom", "repl"), None)),
        check_vma=False,
    )
```
